1024 devices in a mesh: dp: 4 (over x), expert: 64 (over z, y_hi), pipe: 4 (over y_lo, core).
Axes of the slice: x: 4, y: 4 (y_hi: 2, y_lo: 2; y = y_hi * 2 + y_lo), z: 32, core: 2. Of those that a mesh axis runs over, the one named last changes fastest.
Arguments:
- dout: bfloat16 [8192, 4096], P('expert', ('dp', 'pipe')), may hold values from -6 to 6
- expert_ids: int32 [8192, 8], P('expert'), may hold values from 0 to 63, all different within a row; in each aligned block of 128 rows (0 to 127, 128 to 255, ...) at most 20 rows name the same one
- gates: bfloat16 [8192, 8], P('expert'), may hold values from 0.049804688 to 0.5
- down_weight: bfloat16 [64, 1536, 4096], P('expert', None, ('dp', 'pipe')), may hold values from -0.15625 to 0.15625
- hidden_stash: bfloat16 [64, 1280, 1536], P('expert'), may hold values from -0.29882812 to 0.29882812
Outputs:
- hidden_grad: bfloat16 [64, 1280, 1536], P('expert', ('dp', 'pipe'))
- down_grad: bfloat16 [64, 1536, 4096], P('expert', None, ('dp', 'pipe'))
- gate_grad: float32 [8192, 8], P('expert')
The draws below stay inside these ranges and needn't reach their ends.
Inputs may be any that keep to these rules, and one draw needn't show every extreme that they name: `expert_ids`: among the pairs of the 128 tokens of one block no expert is named more than 20 times, and in every draw some expert is named exactly 20 times in some block; the 8 choices of a token differ.
All inputs are finite; a program needn't handle non-finite values.
Results may differ from the reference program's by a relative error of at most 0.022.
Values may be sent and summed in bfloat16 or wider, within the bound.
A program may use at most 32 MiB of HBM per device.

```python
import math
import jax
import jax.numpy as jnp
import numpy as np
from jax import lax

D = 4096
FF = 1536
EXPERTS = 64
TOP = 8
TOK_DEV = 128
CAP = 20
TOKENS = 8192
ROWS = 1280
N_DP = 4
N_EXPERT = 64
N_PIPE = 4


def levels(rng, extent, cuts, smallest, high):
    def one(dim, parts):
        steps = jax.random.uniform(jax.random.fold_in(jax.random.fold_in(rng, 6), dim), (parts,), jnp.float32, smallest / len(cuts), high / len(cuts))
        return jnp.repeat(jnp.exp(steps), extent[dim] // parts).reshape((-1,) + (1,) * (len(extent) - dim - 1))

    loudness = one(*cuts[0])
    for cut in cuts[1:]:
        loudness = loudness * one(*cut)
    return loudness


def deal_out(rng, own, number, rows, amount, top, reach, skew):
    ranking = jax.random.permutation(rng, amount)
    heavy_load, common = portions_of(amount, rows * top, reach, skew, True), portions_of(amount, rows * top, reach, skew, False)
    places = jnp.arange(amount)

    def named(lengths, turn):
        used = int((lengths > 0).sum())
        fixed = max(1, used // 4)
        moved = fixed + (places - fixed + turn * (used - fixed)) % max(1, amount - fixed)
        return jnp.zeros((amount,), jnp.int32).at[ranking[jnp.where(places < fixed, places, moved)]].set(jnp.asarray(lengths, jnp.int32))

    lengths = jnp.where(number % 4 == 0, named(heavy_load, number // 4), named(common, number - number // 4 - 1))
    mixed = jax.random.permutation(jax.random.fold_in(own, 3), amount)
    source_of, taker = mixed[0:amount // 2 * 2:2], mixed[1:amount // 2 * 2:2]
    room = jnp.minimum(lengths[source_of] - 1, reach - lengths[taker]) // 2
    room = jnp.where((source_of == ranking[0]) | (taker == ranking[0]) | (lengths[taker] == 0), 0, jnp.maximum(room, 0))
    moved = jax.random.randint(jax.random.fold_in(own, 4), (amount // 2,), 0, 1 << 20) % (room + 1)
    lengths = lengths.at[source_of].add(-moved).at[taker].add(moved)
    members = jnp.searchsorted(jnp.cumsum(lengths), jnp.arange(rows * top), side="right").astype(jnp.int32)
    grid = members.reshape(top, rows).T
    grid = grid[jax.random.permutation(jax.random.fold_in(own, 1), rows)]
    turn = jax.random.randint(jax.random.fold_in(own, 2), (rows, 1), 0, top)
    return jnp.take_along_axis(grid, (jnp.arange(top)[None, :] + turn) % top, axis=1)


def portions_of(count, total, bound, slope, full):
    loads = [(1 << 20) // math.isqrt(rank ** slope) + 1 for rank in range(1, count + 1)]
    largest = bound if full else min(bound, max(-(-total // count), total * loads[0] // sum(loads)))
    least = 1 if total - largest >= count - 1 else 0
    counts, spare = [largest] + [least] * (count - 1), total - largest - least * (count - 1)
    while spare > 0:
        candidates = [i for i in range(1, count) if counts[i] < largest] or [i for i in range(1, count) if counts[i] < bound]
        whole, left = sum([loads[i] for i in candidates]), spare
        for i in candidates:
            addition = min(bound - counts[i], max(1, left * loads[i] // whole), spare)
            counts[i] = counts[i] + addition
            spare = spare - addition
    return np.array(counts)


def centred(rng, shape, scale, limit, cuts=(), kind=jnp.bfloat16):
    values = scale * jax.random.normal(rng, shape, jnp.float32)
    if cuts:
        values = values * levels(rng, shape, cuts, -0.22, 0.18)
    return jnp.clip(values, -limit, limit).astype(kind)


def setup_inputs(seed: int = 0) -> dict:
    streams_of = jax.random.split(jax.random.key(seed), 6)
    dout = centred(streams_of[0], (TOKENS, D), 1.0, 6.0, ((0, 64), (1, 16)))
    expert_ids_keys = jax.random.split(jax.random.fold_in(streams_of[1], 1), TOKENS // TOK_DEV)
    expert_ids_turns = jax.random.permutation(jax.random.fold_in(streams_of[1], 3), TOKENS // TOK_DEV)
    expert_ids = jax.vmap(lambda own, number: deal_out(jax.random.fold_in(streams_of[1], 2), own, number, TOK_DEV, EXPERTS, TOP, CAP, 2))(expert_ids_keys, expert_ids_turns).reshape((TOKENS, TOP))
    gates = jnp.clip(jnp.exp(math.log(0.5) - 2.306499 * jax.random.uniform(streams_of[2], (TOKENS, TOP), jnp.float32) ** levels(streams_of[2], (TOKENS, TOP), ((0, 64),), -0.2, 0.2)), 0.049804688, 0.5).astype(jnp.bfloat16)
    down_weight = centred(streams_of[3], (EXPERTS, FF, D), FF ** -0.5, 0.15625, ((0, 64), (2, 16)))
    hidden_stash = centred(streams_of[4], (EXPERTS, ROWS, FF), 0.05, 0.29882812, ((0, 64),))
    return {"dout": dout, "expert_ids": expert_ids, "gates": gates, "down_weight": down_weight, "hidden_stash": hidden_stash}


def slot_table(expert_ids):
    flat_ids = expert_ids.reshape(N_EXPERT, TOK_DEV * TOP)
    onehot = (flat_ids[:, :, None] == jnp.arange(EXPERTS, dtype=jnp.int32)[None, None, :]).astype(jnp.int32)
    running = jnp.cumsum(onehot, axis=1)
    slot_index = jnp.sum(running * onehot, axis=2) - 1
    block_index = jnp.arange(N_EXPERT, dtype=jnp.int32)[:, None]
    slot_rows = (block_index * CAP + slot_index).astype(jnp.int32)
    return flat_ids, slot_rows


def reference(dout, expert_ids, gates, down_weight, hidden_stash):
    flat_ids, slot_rows = slot_table(expert_ids)
    pair_number = jnp.arange(TOKENS * TOP, dtype=jnp.int32).reshape(N_EXPERT, TOK_DEV * TOP)
    source_table = jnp.full((EXPERTS, ROWS), -1, dtype=jnp.int32).at[flat_ids, slot_rows].set(pair_number)
    gate_flat = gates.reshape(-1)
    blocks = N_DP * N_PIPE

    def one_expert(operands):
        sources, weight, stash = operands
        filled = sources >= 0
        pair_safe = jnp.maximum(sources, 0).astype(jnp.int32)
        token_safe = (pair_safe // TOP).astype(jnp.int32)
        token_rows = dout[token_safe]
        scale = jnp.where(filled, gate_flat[pair_safe].astype(jnp.float32), 0.0)
        routed = (scale[:, None] * token_rows.astype(jnp.float32)).astype(jnp.bfloat16)
        routed_blocks = routed.astype(jnp.float32).reshape(ROWS, blocks, D // blocks)
        weight_blocks = weight.astype(jnp.float32).reshape(FF, blocks, D // blocks)
        partial_value = jnp.einsum("rbd,fbd->brf", routed_blocks, weight_blocks).astype(jnp.bfloat16)
        partial_value = lax.optimization_barrier(partial_value)
        hidden_grad = jnp.sum(partial_value.astype(jnp.float32), axis=0).astype(jnp.bfloat16)
        down_grad = jnp.dot(stash.T, routed, preferred_element_type=jnp.float32).astype(jnp.bfloat16)
        expert_out = jnp.dot(stash, weight, preferred_element_type=jnp.float32).astype(jnp.bfloat16)
        scores = jnp.sum(token_rows.astype(jnp.float32) * expert_out.astype(jnp.float32), axis=1)
        return hidden_grad, down_grad, scores

    hidden_grad, down_grad, scores = lax.map(one_expert, (source_table, down_weight, hidden_stash))
    gate_grad = scores[flat_ids, slot_rows].reshape(TOKENS, TOP)
    return hidden_grad, down_grad, gate_grad
```

```python
import functools

import jax
import jax.numpy as jnp
from jax import lax
from jax.experimental import pallas as pl
from jax.experimental.pallas import tpu as pltpu
from jax.sharding import PartitionSpec as P

MESH = pl.DeviceIdType.MESH
F32 = jnp.float32
BF16 = jnp.bfloat16
NZ = 32
HALF = NZ // 2
TOK = 128
CAP = 20
ROWS = 4 * CAP
PACK = 48
META = 16
CHUNKS = ((0, 64), (64, 64 + META))


def iota(shape, dim):
    return lax.broadcasted_iota(jnp.int32, shape, dim)


def kernel(
    dout_ref, ids_ref, gates_ref, w_hbm, st_hbm, hg_ref, dg_ref, gg_ref,
    blk, w_v, st_v, rt, ys, yr, eo, pb, cr, xs, xr, yb, srow, rtab, ar,
    load_sem, ring_s, ring_r, y_s, y_r, c_s, c_r, x_s, x_r, b_s, b_r, sc_s, sc_r, ar_s, ar_r,
):
    dp, e, p = lax.axis_index("dp"), lax.axis_index("expert"), lax.axis_index("pipe")
    z, yh = lax.div(e, 2), lax.rem(e, 2)
    yl, core = lax.div(p, 2), lax.rem(p, 2)
    me = dp * 4 + p
    partner = z * 2 + (1 - yh)
    width = w_v.shape[0]
    cols = dout_ref.shape[1]
    halfw = width // 2

    load_w = pltpu.make_async_copy(w_hbm, w_v, load_sem.at[0])
    load_s = pltpu.make_async_copy(st_hbm, st_v, load_sem.at[1])
    load_w.start()
    load_s.start()

    barrier = pltpu.get_barrier_semaphore()

    def greet_expert(b, carry):
        @pl.when(b != e)
        def _():
            pl.semaphore_signal(barrier, inc=1, device_id=(dp, b, p), device_id_type=MESH)
        return carry

    def greet_group(i, carry):
        @pl.when(i != me)
        def _():
            pl.semaphore_signal(
                barrier, inc=1, device_id=(lax.div(i, 4), e, lax.rem(i, 4)), device_id_type=MESH
            )
        return carry

    lax.fori_loop(0, 2 * NZ, greet_expert, 0)
    lax.fori_loop(0, 16, greet_group, 0)

    ids_f = ids_ref[...].astype(F32)
    gates_f = gates_ref[...].astype(F32)
    meta = jnp.concatenate([ids_f, gates_f], axis=0).astype(BF16)
    blk[z, 0:TOK, :] = dout_ref[...]
    blk[z, TOK:TOK + META, 0:128] = meta
    blk[z, TOK:TOK + META, 128:cols] = jnp.zeros((META, cols - 128), BF16)

    pl.semaphore_wait(barrier, 2 * NZ - 1 + 15)

    def ring_copy(d, s, q):
        zz = lax.rem(z - (s - 1) + NZ, NZ) if d == 0 else lax.rem(z + (s - 1), NZ)
        to = lax.rem(z + 1, NZ) if d == 0 else lax.rem(z + NZ - 1, NZ)
        ref = blk.at[zz, pl.ds(*CHUNKS[q])]
        return pltpu.make_async_remote_copy(
            src_ref=ref, dst_ref=ref, send_sem=ring_s.at[d, s - 1, q], recv_sem=ring_r.at[d, s - 1, q],
            device_id=(dp, to * 2 + yh, p), device_id_type=MESH,
        )

    def ring_arrival(d, s, q):
        zz = lax.rem(z - s + NZ, NZ) if d == 0 else lax.rem(z + s, NZ)
        ref = blk.at[zz, pl.ds(*CHUNKS[q])]
        return pltpu.make_async_remote_copy(
            src_ref=ref, dst_ref=ref, send_sem=ring_s.at[d, s - 1, q], recv_sem=ring_r.at[d, s - 1, q],
            device_id=(dp, e, p), device_id_type=MESH,
        )

    for q in range(2):
        for d in range(2):
            ring_copy(d, 1, q).start()

    load_w.wait()
    load_s.wait()

    def out_rows(i, carry):
        r = pl.multiple_of(i * 320, 320)
        prod = jnp.dot(st_v[pl.ds(r, 320), :], w_v[...], preferred_element_type=F32)
        eo[pl.ds(i * 4, 4)] = prod.reshape(4, ROWS, cols)
        return carry

    lax.fori_loop(0, 4, out_rows, 0)

    lower_tri = (iota((TOK, TOK), 0) < iota((TOK, TOK), 1)).astype(F32).astype(BF16)
    rows80 = iota((ROWS, TOK), 0).astype(F32)
    rows48 = iota((PACK, TOK), 0).astype(F32)
    c_id, r_id = iota((ROWS, PACK), 1), iota((ROWS, PACK), 0)
    spot = jnp.where(c_id < CAP, c_id, c_id + CAP) + (1 - yh) * CAP
    place = jnp.where((c_id < 2 * CAP) & (spot == r_id), 1.0, 0.0).astype(BF16)
    yh_f = (yh * CAP).astype(F32)

    def group_of(s):
        up = lax.rem(z + s, 2) == 1
        low = jnp.where(up, lax.rem(z + s - 1, NZ), lax.rem(z - s + NZ, NZ))
        return lax.div(low, 2)

    def receive(s):
        for q in range(2):
            for d in range(2):
                def take():
                    ring_arrival(d, s, q).wait_recv()

                    @pl.when(s < (HALF if q == d else HALF - 1))
                    def _():
                        ring_copy(d, s + 1, q).start()

                if q == d:
                    take()
                else:
                    pl.when(s < HALF)(take)

    def y_copy(g):
        return pltpu.make_async_remote_copy(
            src_ref=ys.at[g], dst_ref=yr.at[g], send_sem=y_s.at[g], recv_sem=y_r.at[g],
            device_id=(dp, partner, p), device_id_type=MESH,
        )

    def select(s):
        g = group_of(s)
        x = blk[pl.ds(2 * g, 2), 0:TOK, :].reshape(2 * TOK, cols)
        match, gate = [], []
        for name in (e, partner):
            for j in range(2):
                m16 = blk[2 * g + j, TOK:TOK + META, 0:128].astype(F32)
                hit = m16[0:8] == name.astype(F32)
                match.append(jnp.sum(jnp.where(hit, 1.0, 0.0), axis=0, keepdims=True))
                gate.append(jnp.sum(jnp.where(hit, m16[8:16], 0.0), axis=0, keepdims=True))
        counts = jnp.dot(
            jnp.concatenate(match + [jnp.zeros((12, TOK), F32)], axis=0).astype(BF16),
            lower_tri, preferred_element_type=F32,
        )
        own, theirs = [], []
        for j in range(2):
            key = jnp.where(match[j] > 0.5, counts[j:j + 1] + (2.0 * j * CAP + yh_f), -1.0)
            own.append(jnp.where(rows80 == key, gate[j], 0.0))
            key = jnp.where(match[2 + j] > 0.5, counts[2 + j:3 + j] + 1.0 * j * CAP, -1.0)
            theirs.append(jnp.where(rows48 == key, gate[2 + j], 0.0))
        both = jnp.concatenate(
            [jnp.concatenate(own, axis=1), jnp.concatenate(theirs, axis=1)], axis=0
        ).astype(BF16)
        picked = jnp.dot(both, x, preferred_element_type=F32).astype(BF16)
        ys[g] = picked[ROWS:]
        y_copy(g).start()
        rt[g] = picked[:ROWS]

    def core_copy(g):
        h = lax.div(g, 2)
        return pltpu.make_async_remote_copy(
            src_ref=pb.at[g], dst_ref=cr.at[h], send_sem=c_s.at[h], recv_sem=c_r.at[h],
            device_id=(dp, e, yl * 2 + (1 - core)), device_id_type=MESH,
        )

    def score_copy(g, b):
        return pltpu.make_async_remote_copy(
            src_ref=srow.at[g], dst_ref=rtab.at[e], send_sem=sc_s, recv_sem=sc_r,
            device_id=(dp, b, p), device_id_type=MESH,
        )

    diagonal = iota((ROWS, 128), 0) == iota((ROWS, 128), 1)

    def multiply(s):
        g = group_of(s)
        y_copy(g).wait_recv()
        rr = (
            rt[g].astype(F32) + jnp.dot(place, yr[g], preferred_element_type=F32)
        ).astype(BF16)
        rt[g] = rr
        for n in range(width // 256):
            part = lax.dot_general(
                rr, w_v[n * 256:(n + 1) * 256, :], (((1,), (1,)), ((), ())),
                preferred_element_type=F32,
            )
            pb[g, :, n * 256:(n + 1) * 256] = part.astype(BF16)

        @pl.when(lax.rem(g, 2) != core)
        def _():
            core_copy(g).start()

        total = jnp.sum(rr.astype(F32) * eo[g], axis=1, keepdims=True)
        srow[g] = jnp.sum(jnp.where(diagonal, total, 0.0), axis=0, keepdims=True)
        for j in range(4):
            b = 4 * g + j

            @pl.when(b != e)
            def _():
                score_copy(g, b).start()

            @pl.when(b == e)
            def _():
                rtab[e] = srow[g]

    def x_copy(h, side, lo, size):
        to = lax.rem(dp + 1, 4) if side == 0 else lax.rem(dp + 3, 4)
        part = pl.ds(lo, size)
        return pltpu.make_async_remote_copy(
            src_ref=xs.at[h, :, part], dst_ref=xr.at[side, h, :, part],
            send_sem=x_s.at[side, h], recv_sem=x_r.at[side, h],
            device_id=(to, e, p), device_id_type=MESH,
        )

    b_copy = pltpu.make_async_remote_copy(
        src_ref=xs.at[lax.div(dp * 4 + 2 * (1 - yl) + core, 2)], dst_ref=yb, send_sem=b_s, recv_sem=b_r,
        device_id=(dp, e, 2 * (1 - yl) + core), device_id_type=MESH,
    )

    def add_up(dst, g, extra):
        h = lax.div(g, 2)
        for n in range(4):
            c = slice(n * (width // 4), (n + 1) * (width // 4))
            t = pb[g, :, c].astype(F32) + cr[h, :, c].astype(F32)
            for side, lo, hi in extra:
                if lo <= n * (width // 4) < hi:
                    t = t + xr[side, h, :, c].astype(F32)
            dst(c, t)

    def send_dst(h):
        def put(c, t):
            xs[h, :, c] = t.astype(BF16)
        return put

    def far(s):
        g = group_of(s)
        h = lax.div(g, 2)
        mine = lax.rem(g, 2) == core
        away = lax.rem(dp - lax.div(g, 4) + 4, 4)

        @pl.when(mine)
        def _():
            core_copy(g).wait_recv()

        @pl.when(mine & (away == 2))
        def _():
            add_up(send_dst(h), g, ())
            x_copy(h, 0, 0, halfw).start()
            x_copy(h, 1, halfw, halfw).start()

    def near(s):
        g = group_of(s)
        h = lax.div(g, 2)
        mine = lax.rem(g, 2) == core
        away = lax.rem(dp - lax.div(g, 4) + 4, 4)

        @pl.when(mine & (away == 1))
        def _():
            x_copy(h, 1, halfw, halfw).wait_recv()
            add_up(send_dst(h), g, ((1, halfw, width),))
            x_copy(h, 1, 0, width).start()

        @pl.when(mine & (away == 3))
        def _():
            x_copy(h, 0, 0, halfw).wait_recv()
            add_up(send_dst(h), g, ((0, 0, halfw),))
            x_copy(h, 0, 0, width).start()

    def column(s):
        g = group_of(s)
        h = lax.div(g, 2)
        mine = lax.rem(g, 2) == core
        away = lax.rem(dp - lax.div(g, 4) + 4, 4)

        @pl.when(mine & (away == 0))
        def _():
            x_copy(h, 0, 0, width).wait_recv()
            x_copy(h, 1, 0, width).wait_recv()

            @pl.when(lax.div(lax.rem(g, 4), 2) != yl)
            def _():
                add_up(send_dst(h), g, ((0, 0, width), (1, 0, width)))
                b_copy.start()

    last = HALF + 1

    def body(s, carry):
        @pl.when(s <= HALF)
        def _():
            receive(s)
            select(s)

        @pl.when(s >= 2)
        def _():
            multiply(s - 1)

        @pl.when(s >= 3)
        def _():
            far(s - 2)

        @pl.when(s >= 4)
        def _():
            near(s - 3)

        @pl.when(s >= 5)
        def _():
            column(s - 4)

        return carry

    lax.fori_loop(1, last + 1, body, 0)

    def down(lo, hi):
        for n in range(lo, hi):
            part = lax.dot_general(
                st_v[:, n * 256:(n + 1) * 256], rt[...].reshape(16 * ROWS, cols),
                (((0,), (0,)), ((), ())), preferred_element_type=F32,
            )
            dg_ref[0, n * 256:(n + 1) * 256, :] = part.astype(BF16)

    far(HALF)
    near(HALF - 1)
    column(HALF - 2)
    down(0, 3)
    near(HALF)
    column(HALF - 1)
    down(3, 6)
    column(HALF)

    pltpu.make_async_copy(
        rtab.at[pl.ds(0, 2 * NZ - 1)], rtab.at[pl.ds(0, 2 * NZ - 1)], sc_r
    ).wait()
    table = rtab[...].reshape(2 * NZ, 128)
    high = table.astype(BF16)
    low = (table - high.astype(F32)).astype(BF16)
    names = iota((2 * NZ, TOK), 0)
    hits = [jnp.where(names == ids_ref[k:k + 1, :], 1.0, 0.0) for k in range(8)]
    named = functools.reduce(lambda a, b: a + b, hits)
    counts = jnp.dot(named.astype(BF16), lower_tri, preferred_element_type=F32)
    lanes = iota((128, TOK), 0).astype(F32)
    first = (lax.rem(e, 4) * CAP).astype(F32)
    out = []
    for k in range(8):
        slot = jnp.sum(hits[k] * counts, axis=0, keepdims=True) + first
        one = hits[k].astype(BF16)
        values = lax.dot_general(
            high, one, (((0,), (0,)), ((), ())), preferred_element_type=F32
        ) + lax.dot_general(low, one, (((0,), (0,)), ((), ())), preferred_element_type=F32)
        out.append(jnp.sum(jnp.where(lanes == slot, values, 0.0), axis=0, keepdims=True))
    ar[me] = jnp.concatenate(out, axis=0)

    def spread(i):
        return pltpu.make_async_remote_copy(
            src_ref=ar.at[me], dst_ref=ar.at[me], send_sem=ar_s, recv_sem=ar_r,
            device_id=(lax.div(i, 4), e, lax.rem(i, 4)), device_id_type=MESH,
        )

    def spread_one(i, carry):
        @pl.when(i != me)
        def _():
            spread(i).start()
        return carry

    lax.fori_loop(0, 16, spread_one, 0)

    b_copy.wait_recv()

    def final(c, t):
        hg_ref[0, :, c] = (t + yb[:, c].astype(F32)).astype(BF16)

    add_up(final, me, ((0, 0, width), (1, 0, width)))

    pltpu.make_async_copy(ar.at[pl.ds(0, 15)], ar.at[pl.ds(0, 15)], ar_r).wait()
    gg_ref[...] = jnp.sum(ar[...], axis=0) / gates_f

    def ring_sent(s, carry):
        for q in range(2):
            for d in range(2):
                if q == d:
                    ring_copy(d, s, q).wait_send()
                else:
                    pl.when(s < HALF)(lambda d=d, q=q: ring_copy(d, s, q).wait_send())
        y_copy(s - 1).wait_send()

        g = s - 1
        h = lax.div(g, 2)
        mine = lax.rem(g, 2) == core
        away = lax.rem(dp - lax.div(g, 4) + 4, 4)

        @pl.when(jnp.logical_not(mine))
        def _():
            core_copy(g).wait_send()

        @pl.when(mine & (away == 2))
        def _():
            x_copy(h, 0, 0, halfw).wait_send()
            x_copy(h, 1, halfw, halfw).wait_send()

        @pl.when(mine & (away == 1))
        def _():
            x_copy(h, 1, 0, width).wait_send()

        @pl.when(mine & (away == 3))
        def _():
            x_copy(h, 0, 0, width).wait_send()

        return carry

    lax.fori_loop(1, HALF + 1, ring_sent, 0)
    b_copy.wait_send()
    pltpu.make_async_copy(
        rtab.at[pl.ds(0, 2 * NZ - 1)], rtab.at[pl.ds(0, 2 * NZ - 1)], sc_s
    ).wait()
    pltpu.make_async_copy(ar.at[pl.ds(0, 15)], ar.at[pl.ds(0, 15)], ar_s).wait()


def local(dout, expert_ids, gates, down_weight, hidden_stash):
    _, width, cols = down_weight.shape
    slots = hidden_stash.shape[1]
    vmem = pl.BlockSpec(memory_space=pltpu.VMEM)
    hbm = pl.BlockSpec(memory_space=pl.ANY)
    dma = pltpu.SemaphoreType.DMA
    hg, dg, gg = pl.pallas_call(
        kernel,
        out_shape=(
            jax.ShapeDtypeStruct((1, ROWS, width), BF16),
            jax.ShapeDtypeStruct((1, width, cols), BF16),
            jax.ShapeDtypeStruct((8, TOK), F32),
        ),
        in_specs=[vmem, vmem, vmem, hbm, hbm],
        out_specs=(vmem, vmem, vmem),
        scratch_shapes=[
            pltpu.VMEM((NZ, TOK + META, cols), BF16),
            pltpu.VMEM((width, cols), BF16),
            pltpu.VMEM((slots, width), BF16),
            pltpu.VMEM((16, ROWS, cols), BF16),
            pltpu.VMEM((16, PACK, cols), BF16),
            pltpu.VMEM((16, PACK, cols), BF16),
            pltpu.VMEM((16, ROWS, cols), F32),
            pltpu.VMEM((16, ROWS, width), BF16),
            pltpu.VMEM((8, ROWS, width), BF16),
            pltpu.VMEM((8, ROWS, width), BF16),
            pltpu.VMEM((2, 8, ROWS, width), BF16),
            pltpu.VMEM((ROWS, width), BF16),
            pltpu.VMEM((16, 1, 128), F32),
            pltpu.VMEM((2 * NZ, 1, 128), F32),
            pltpu.VMEM((16, 8, TOK), F32),
            dma((2,)),
            dma((2, HALF, 2)),
            dma((2, HALF, 2)),
            dma((16,)),
            dma((16,)),
            dma((8,)),
            dma((8,)),
            dma((2, 8)),
            dma((2, 8)),
            dma(()),
            dma(()),
            dma(()),
            dma(()),
            dma(()),
            dma(()),
        ],
        compiler_params=pltpu.CompilerParams(
            collective_id=0, has_side_effects=True, vmem_limit_bytes=52 * 2**20
        ),
        cost_estimate=pl.CostEstimate(
            flops=6 * slots * width * cols, bytes_accessed=6 * 2**20, transcendentals=0
        ),
    )(dout, expert_ids.T, gates.T, down_weight[0], hidden_stash[0])
    return hg, dg, gg.T


def solution(mesh):
    in_specs = (
        P("expert", ("dp", "pipe")),
        P("expert", None),
        P("expert", None),
        P("expert", None, ("dp", "pipe")),
        P("expert", None, None),
    )
    out_specs = (
        P("expert", ("dp", "pipe"), None),
        P("expert", None, ("dp", "pipe")),
        P("expert", None),
    )
    return jax.shard_map(local, mesh=mesh, in_specs=in_specs, out_specs=out_specs, check_vma=False)
```

```python
import functools

import jax
import jax.numpy as jnp
from jax import lax
from jax.experimental import pallas as pl
from jax.experimental.pallas import tpu as pltpu
from jax.sharding import PartitionSpec as P

MESH = pl.DeviceIdType.MESH
F32 = jnp.float32
BF16 = jnp.bfloat16
PAIRS = 16
NAMES = 4 * PAIRS
TOK = 128
CAP = 20
ROWS = 4 * CAP
SEG = 24
PACK = 2 * SEG
META = 16
BLOCK = 2 * TOK + META


def iota(shape, dim):
    return lax.broadcasted_iota(jnp.int32, shape, dim)


def kernel(
    dout_hbm, meta_hbm, w_hbm, st_hbm, hg_ref, dg_ref, gg_ref,
    src, w_v, st_v, sbuf, rbuf, rt, eo, pb, cr, xs, yb, xr, srow, rtab, ar,
    load_sem, ch_s, ch_r, f_s, f_r, c_s, c_r, y_s, y_r, x_s, x_r, sc_s, sc_r, ar_s, ar_r,
):
    dp, e, p = lax.axis_index("dp"), lax.axis_index("expert"), lax.axis_index("pipe")
    pair, quad = lax.div(e, 4), lax.rem(e, 4)
    yl, core = lax.div(p, 2), lax.rem(p, 2)
    me = dp * 4 + p
    width, cols = w_v.shape
    half = cols // 2

    def at_pair(d):
        return lax.rem(pair + d + PAIRS, PAIRS)

    loads = [
        pltpu.make_async_copy(dout_hbm.at[:, pl.ds(0, half)], src.at[0, pl.ds(0, TOK)], load_sem.at[0]),
        pltpu.make_async_copy(dout_hbm.at[:, pl.ds(half, half)], src.at[0, pl.ds(TOK, TOK)], load_sem.at[1]),
        pltpu.make_async_copy(meta_hbm, src.at[0, pl.ds(2 * TOK, META)], load_sem.at[2]),
        pltpu.make_async_copy(w_hbm, w_v, load_sem.at[3]),
        pltpu.make_async_copy(st_hbm, st_v, load_sem.at[4]),
    ]
    for copy in loads:
        copy.start()

    barrier = pltpu.get_barrier_semaphore()

    def greet(name):
        pl.semaphore_signal(barrier, inc=1, device_id=(dp, name, p), device_id_type=MESH)

    greet(at_pair(4) * 4 + quad)
    greet(at_pair(-4) * 4 + quad)

    def greet_near(k, carry):
        name = at_pair(lax.div(k, 4) - 2) * 4 + lax.rem(k, 4)

        @pl.when(name != e)
        def _():
            greet(name)
        return carry

    def greet_group(i, carry):
        @pl.when(i != me)
        def _():
            pl.semaphore_signal(
                barrier, inc=1, device_id=(lax.div(i, 4), e, lax.rem(i, 4)), device_id_type=MESH
            )
        return carry

    lax.fori_loop(0, 16, greet_near, 0)
    lax.fori_loop(0, 16, greet_group, 0)
    for copy in loads[:3]:
        copy.wait()
    pl.semaphore_wait(barrier, 2 + 15 + 15)

    def chain(i):
        frm, to = ((0, -4), (0, 4), (1, -4))[i - 1]
        return pltpu.make_async_remote_copy(
            src_ref=src.at[frm], dst_ref=src.at[i], send_sem=ch_s.at[i - 1], recv_sem=ch_r.at[i - 1],
            device_id=(dp, at_pair(to) * 4 + quad, p), device_id_type=MESH,
        )

    chain(1).start()
    chain(2).start()

    lower_tri = (iota((TOK, TOK), 0) < iota((TOK, TOK), 1)).astype(F32).astype(BF16)
    segment = iota((SEG, TOK), 0).astype(F32)
    row16 = iota((16, TOK), 0)
    names16 = (
        ((row16 >> 2) + (pair + PAIRS - 1)) % PAIRS * 4 + (row16 & 3)
    ).astype(F32)
    shift = (0, 4, -4, 8)

    def fill(i, k, g):
        name = at_pair(lax.div(k, 4) - 1) * 4 + lax.rem(k, 4)
        return name, pltpu.make_async_remote_copy(
            src_ref=sbuf.at[i, k], dst_ref=rbuf.at[g, quad], send_sem=f_s.at[i], recv_sem=f_r.at[g],
            device_id=(dp, name, p), device_id_type=MESH,
        )

    def select(i):
        g = at_pair(shift[i])
        x = jnp.concatenate([src[i, 0:TOK, :], src[i, TOK:2 * TOK, :]], axis=1)
        m16 = src[i, 2 * TOK:BLOCK, :].astype(F32)
        match = jnp.zeros((16, TOK), F32)
        gate = jnp.zeros((16, TOK), F32)
        for k in range(8):
            hit = m16[k:k + 1] == names16
            match = match + jnp.where(hit, 1.0, 0.0)
            gate = gate + jnp.where(hit, m16[8 + k:9 + k], 0.0)
        counts = jnp.dot(match.astype(BF16), lower_tri, preferred_element_type=F32)
        key = jnp.where(match > 0.5, counts, -1.0)
        pick = jnp.concatenate(
            [jnp.where(segment == key[k:k + 1], gate[k:k + 1], 0.0) for k in range(16)], axis=0
        ).astype(BF16)
        rows = jnp.dot(pick, x, preferred_element_type=F32)
        for k in range(16):
            r = rows[k * SEG:(k + 1) * SEG]
            sbuf[i, k] = jnp.concatenate([r[:, :half], r[:, half:]], axis=0).astype(BF16)

        def send(k, carry):
            name, copy = fill(i, k, g)

            @pl.when(name != e)
            def _():
                copy.start()
            return carry

        lax.fori_loop(0, 16, send, 0)
        pltpu.make_async_copy(sbuf.at[i, 4 + quad], rbuf.at[g, quad], f_r.at[g]).start()

    select(0)

    for copy in loads[3:]:
        copy.wait()

    def out_rows(i, carry):
        r = pl.multiple_of(i * 320, 320)
        prod = jnp.dot(st_v[pl.ds(r, 320), :], w_v[...], preferred_element_type=F32)
        eo[pl.ds(i * 4, 4)] = prod.reshape(4, ROWS, cols)
        return carry

    lax.fori_loop(0, 4, out_rows, 0)

    c_id, r_id = iota((2 * ROWS, 4 * PACK), 1), iota((2 * ROWS, 4 * PACK), 0)
    block = (
        (c_id >= PACK).astype(jnp.int32) + (c_id >= 2 * PACK).astype(jnp.int32)
        + (c_id >= 3 * PACK).astype(jnp.int32)
    )
    inside = c_id - block * PACK
    right = (inside >= SEG).astype(jnp.int32)
    slot_id = inside - right * SEG
    place = jnp.where(
        (slot_id < CAP) & (right * ROWS + block * CAP + slot_id == r_id), 1.0, 0.0
    ).astype(BF16)

    def group_of(j):
        i, r = lax.div(j, 4), lax.rem(j, 4)
        delta = jnp.where(r == 2, -1, jnp.where(r == 3, 2, r))
        off = jnp.where(i == 1, 4, jnp.where(i == 2, -4, jnp.where(i == 3, 8, 0)))
        return lax.rem(pair - delta + off + 2 * PAIRS, PAIRS)

    def core_copy(g):
        h = lax.div(g, 2)
        return pltpu.make_async_remote_copy(
            src_ref=pb.at[g], dst_ref=cr.at[h], send_sem=c_s.at[h], recv_sem=c_r.at[h],
            device_id=(dp, e, yl * 2 + (1 - core)), device_id_type=MESH,
        )

    def score_copy(g, b):
        return pltpu.make_async_remote_copy(
            src_ref=srow.at[g], dst_ref=rtab.at[e], send_sem=sc_s, recv_sem=sc_r,
            device_id=(dp, b, p), device_id_type=MESH,
        )

    diagonal = iota((ROWS, 128), 0) == iota((ROWS, 128), 1)

    def multiply(j):
        g = group_of(j)
        pltpu.make_async_copy(rbuf.at[g], rbuf.at[g], f_r.at[g]).wait()
        both = jnp.dot(place, rbuf[g].reshape(4 * PACK, half), preferred_element_type=F32)
        rr = jnp.concatenate([both[:ROWS], both[ROWS:]], axis=1).astype(BF16)
        rt[g] = rr
        for n in range(width // 256):
            part = lax.dot_general(
                rr, w_v[n * 256:(n + 1) * 256, :], (((1,), (1,)), ((), ())),
                preferred_element_type=F32,
            )
            pb[g, :, n * 256:(n + 1) * 256] = part.astype(BF16)

        @pl.when(lax.rem(g, 2) != core)
        def _():
            core_copy(g).start()

        total = jnp.sum(rr.astype(F32) * eo[g], axis=1, keepdims=True)
        srow[g] = jnp.sum(jnp.where(diagonal, total, 0.0), axis=0, keepdims=True)
        for q in range(4):
            b = 4 * g + q

            @pl.when(b != e)
            def _():
                score_copy(g, b).start()

            @pl.when(b == e)
            def _():
                rtab[e] = srow[g]

    def y_copy(h):
        return pltpu.make_async_remote_copy(
            src_ref=xs.at[h], dst_ref=yb.at[h], send_sem=y_s.at[h], recv_sem=y_r.at[h],
            device_id=(dp, e, (1 - yl) * 2 + core), device_id_type=MESH,
        )

    def x_copy(g):
        owner = lax.div(g, 4)
        place_x = jnp.maximum(lax.rem(dp - owner + 4, 4) - 1, 0)
        h = lax.div(g, 2)
        return pltpu.make_async_remote_copy(
            src_ref=xs.at[h], dst_ref=xr.at[place_x], send_sem=x_s.at[h], recv_sem=x_r.at[place_x],
            device_id=(owner, e, p), device_id_type=MESH,
        )

    def roles(g):
        mine = lax.rem(g, 2) == core
        row = lax.div(lax.rem(g, 4), 2) == yl
        return mine & jnp.logical_not(row), mine & row, mine & row & (lax.div(g, 4) != dp)

    step = width // 4

    def put_down(h, refs):
        for n in range(4):
            c = slice(n * step, (n + 1) * step)
            t = refs[0][:, c].astype(F32)
            for ref in refs[1:]:
                t = t + ref[:, c].astype(F32)
            xs[h, :, c] = t.astype(BF16)

    def along_y(j):
        g = group_of(j)
        h = lax.div(g, 2)
        gives, _, _ = roles(g)

        @pl.when(gives)
        def _():
            core_copy(g).wait_recv()
            put_down(h, (pb.at[g], cr.at[h]))
            y_copy(h).start()

    def along_x(j):
        g = group_of(j)
        h = lax.div(g, 2)
        _, keeps, passes = roles(g)

        @pl.when(keeps)
        def _():
            core_copy(g).wait_recv()
            y_copy(h).wait_recv()

        @pl.when(passes)
        def _():
            put_down(h, (pb.at[g], cr.at[h], yb.at[h]))
            x_copy(g).start()

    def body(j, carry):
        @pl.when(j == 4)
        def _():
            along_y(j - 1)
            chain(1).wait_recv()
            chain(3).start()
            select(1)
            chain(2).wait_recv()
            select(2)

        @pl.when(j == 8)
        def _():
            along_y(j - 1)
            chain(3).wait_recv()
            select(3)

        multiply(j)

        @pl.when((j != 0) & (j != 4) & (j != 8))
        def _():
            along_y(j - 1)

        @pl.when(j >= 4)
        def _():
            along_x(j - 4)

        return carry

    lax.fori_loop(0, 16, body, 0)

    def down(lo, hi):
        for n in range(lo, hi):
            part = lax.dot_general(
                st_v[:, n * 256:(n + 1) * 256], rt[...].reshape(16 * ROWS, cols),
                (((0,), (0,)), ((), ())), preferred_element_type=F32,
            )
            dg_ref[0, n * 256:(n + 1) * 256, :] = part.astype(BF16)

    along_y(15)
    down(0, 3)
    along_x(12)
    along_x(13)
    down(3, 6)
    along_x(14)
    along_x(15)

    m16 = src[0, 2 * TOK:BLOCK, :].astype(F32)
    names = iota((NAMES, TOK), 0).astype(F32)
    hits = [jnp.where(names == m16[k:k + 1, :], 1.0, 0.0) for k in range(8)]
    named = functools.reduce(lambda a, b: a + b, hits)
    counts = jnp.dot(named.astype(BF16), lower_tri, preferred_element_type=F32)
    lanes = iota((128, TOK), 0).astype(F32)
    first = (quad * CAP).astype(F32)
    pltpu.make_async_copy(
        rtab.at[pl.ds(0, NAMES - 1)], rtab.at[pl.ds(0, NAMES - 1)], sc_r
    ).wait()
    table = rtab[...].reshape(NAMES, 128)
    high = table.astype(BF16)
    low = (table - high.astype(F32)).astype(BF16)
    out = []
    for k in range(8):
        slot = jnp.sum(hits[k] * counts, axis=0, keepdims=True) + first
        one = hits[k].astype(BF16)
        values = lax.dot_general(
            high, one, (((0,), (0,)), ((), ())), preferred_element_type=F32
        ) + lax.dot_general(low, one, (((0,), (0,)), ((), ())), preferred_element_type=F32)
        out.append(jnp.sum(jnp.where(lanes == slot, values, 0.0), axis=0, keepdims=True))
    ar[me] = jnp.concatenate(out, axis=0)

    def spread_one(i, carry):
        @pl.when(i != me)
        def _():
            pltpu.make_async_remote_copy(
                src_ref=ar.at[me], dst_ref=ar.at[me], send_sem=ar_s, recv_sem=ar_r,
                device_id=(lax.div(i, 4), e, lax.rem(i, 4)), device_id_type=MESH,
            ).start()
        return carry

    lax.fori_loop(0, 16, spread_one, 0)

    for i in range(3):
        pltpu.make_async_copy(xr.at[i], xr.at[i], x_r.at[i]).wait()
    h = lax.div(me, 2)
    for n in range(4):
        c = slice(n * step, (n + 1) * step)
        t = pb[me, :, c].astype(F32)
        for ref in (cr.at[h], yb.at[h], xr.at[0], xr.at[1], xr.at[2]):
            t = t + ref[:, c].astype(F32)
        hg_ref[0, :, c] = t.astype(BF16)

    pltpu.make_async_copy(ar.at[pl.ds(0, 15)], ar.at[pl.ds(0, 15)], ar_r).wait()
    gg_ref[...] = jnp.sum(ar[...], axis=0) / m16[8:16]

    for i in range(1, 4):
        chain(i).wait_send()
    for i in range(4):
        pltpu.make_async_copy(sbuf.at[i, pl.ds(0, 15)], sbuf.at[i, pl.ds(0, 15)], f_s.at[i]).wait()

    def sent(g, carry):
        gives, _, passes = roles(g)

        @pl.when(lax.rem(g, 2) != core)
        def _():
            core_copy(g).wait_send()

        @pl.when(gives)
        def _():
            y_copy(lax.div(g, 2)).wait_send()

        @pl.when(passes)
        def _():
            x_copy(g).wait_send()

        return carry

    lax.fori_loop(0, 16, sent, 0)
    pltpu.make_async_copy(
        rtab.at[pl.ds(0, NAMES - 1)], rtab.at[pl.ds(0, NAMES - 1)], sc_s
    ).wait()
    pltpu.make_async_copy(ar.at[pl.ds(0, 15)], ar.at[pl.ds(0, 15)], ar_s).wait()


def local(dout, expert_ids, gates, down_weight, hidden_stash):
    _, width, cols = down_weight.shape
    slots = hidden_stash.shape[1]
    vmem = pl.BlockSpec(memory_space=pltpu.VMEM)
    hbm = pl.BlockSpec(memory_space=pl.ANY)
    dma = pltpu.SemaphoreType.DMA
    meta = jnp.concatenate([expert_ids.T.astype(BF16), gates.T], axis=0)
    hg, dg, gg = pl.pallas_call(
        kernel,
        out_shape=(
            jax.ShapeDtypeStruct((1, ROWS, width), BF16),
            jax.ShapeDtypeStruct((1, width, cols), BF16),
            jax.ShapeDtypeStruct((8, TOK), F32),
        ),
        in_specs=[hbm, hbm, hbm, hbm],
        out_specs=(vmem, vmem, vmem),
        scratch_shapes=[
            pltpu.VMEM((4, BLOCK, cols // 2), BF16),
            pltpu.VMEM((width, cols), BF16),
            pltpu.VMEM((slots, width), BF16),
            pltpu.VMEM((4, 16, PACK, cols // 2), BF16),
            pltpu.VMEM((PAIRS, 4, PACK, cols // 2), BF16),
            pltpu.VMEM((16, ROWS, cols), BF16),
            pltpu.VMEM((16, ROWS, cols), F32),
            pltpu.VMEM((16, ROWS, width), BF16),
            pltpu.VMEM((8, ROWS, width), BF16),
            pltpu.VMEM((8, ROWS, width), BF16),
            pltpu.VMEM((8, ROWS, width), BF16),
            pltpu.VMEM((3, ROWS, width), BF16),
            pltpu.VMEM((16, 1, 128), F32),
            pltpu.VMEM((NAMES, 1, 128), F32),
            pltpu.VMEM((16, 8, TOK), F32),
            dma((5,)),
            dma((3,)),
            dma((3,)),
            dma((4,)),
            dma((16,)),
            dma((8,)),
            dma((8,)),
            dma((8,)),
            dma((8,)),
            dma((8,)),
            dma((3,)),
            dma(()),
            dma(()),
            dma(()),
            dma(()),
        ],
        compiler_params=pltpu.CompilerParams(
            collective_id=0, has_side_effects=True, vmem_limit_bytes=60 * 2**20
        ),
        cost_estimate=pl.CostEstimate(
            flops=6 * slots * width * cols, bytes_accessed=6 * 2**20, transcendentals=0
        ),
    )(dout, meta, down_weight[0], hidden_stash[0])
    return hg, dg, gg.T


def solution(mesh):
    in_specs = (
        P("expert", ("dp", "pipe")),
        P("expert", None),
        P("expert", None),
        P("expert", None, ("dp", "pipe")),
        P("expert", None, None),
    )
    out_specs = (
        P("expert", ("dp", "pipe"), None),
        P("expert", None, ("dp", "pipe")),
        P("expert", None),
    )
    return jax.shard_map(local, mesh=mesh, in_specs=in_specs, out_specs=out_specs, check_vma=False)
```

```python
import functools

import jax
import jax.numpy as jnp
from jax import lax
from jax.experimental import pallas as pl
from jax.experimental.pallas import tpu as pltpu
from jax.sharding import PartitionSpec as P

MESH = pl.DeviceIdType.MESH
F32 = jnp.float32
BF16 = jnp.bfloat16
PAIRS = 16
NAMES = 4 * PAIRS
TOK = 128
CAP = 20
ROWS = 4 * CAP
SEG = 24
PACK = 2 * SEG
META = 16
BLOCK = 2 * TOK + META


def iota(shape, dim):
    return lax.broadcasted_iota(jnp.int32, shape, dim)


def kernel(
    dout_hbm, meta_hbm, w_hbm, st_hbm, hg_ref, dg_ref, gg_ref,
    src, w_v, st_v, sbuf, rbuf, rt, eo, pb, cr, xs, yb, xr, acc, srow, rtab, ar,
    load_sem, ch_s, ch_r, f_s, f_r, c_s, c_r, y_s, y_r, x_s, x_r, sc_s, sc_r, ar_s, ar_r,
):
    dp, e, p = lax.axis_index("dp"), lax.axis_index("expert"), lax.axis_index("pipe")
    pair, quad = lax.div(e, 4), lax.rem(e, 4)
    yh, yl, core = lax.rem(e, 2), lax.div(p, 2), lax.rem(p, 2)
    me = dp * 4 + p
    width, cols = w_v.shape
    half = cols // 2

    def at_pair(d):
        return lax.rem(pair + d + PAIRS, PAIRS)

    loads = [
        pltpu.make_async_copy(dout_hbm.at[:, pl.ds(0, half)], src.at[0, pl.ds(0, TOK)], load_sem.at[0]),
        pltpu.make_async_copy(dout_hbm.at[:, pl.ds(half, half)], src.at[0, pl.ds(TOK, TOK)], load_sem.at[1]),
        pltpu.make_async_copy(meta_hbm, src.at[0, pl.ds(2 * TOK, META)], load_sem.at[2]),
        pltpu.make_async_copy(w_hbm, w_v, load_sem.at[3]),
        pltpu.make_async_copy(st_hbm, st_v, load_sem.at[4]),
    ]
    for copy in loads:
        copy.start()

    barrier = pltpu.get_barrier_semaphore()

    def greet(name):
        pl.semaphore_signal(barrier, inc=1, device_id=(dp, name, p), device_id_type=MESH)

    greet(at_pair(4) * 4 + quad)
    greet(at_pair(-4) * 4 + quad)

    def greet_near(k, carry):
        name = at_pair(lax.div(k, 4) - 2 + yh) * 4 + lax.rem(k, 4)

        @pl.when(name != e)
        def _():
            greet(name)
        return carry

    def greet_group(i, carry):
        @pl.when(i != me)
        def _():
            pl.semaphore_signal(
                barrier, inc=1, device_id=(lax.div(i, 4), e, lax.rem(i, 4)), device_id_type=MESH
            )
        return carry

    lax.fori_loop(0, 16, greet_near, 0)
    lax.fori_loop(0, 16, greet_group, 0)
    for copy in loads[:3]:
        copy.wait()
    pl.semaphore_wait(barrier, 2 + 15 + 15)

    def chain(i):
        frm, to, dst, lo, size = (
            (0, -4, 1, 0, BLOCK), (0, 4, 2, 0, BLOCK),
            (1, -4, 3, TOK, BLOCK - TOK), (2, 4, 3, 0, TOK),
        )[i - 1]
        return pltpu.make_async_remote_copy(
            src_ref=src.at[frm, pl.ds(lo, size)], dst_ref=src.at[dst, pl.ds(lo, size)],
            send_sem=ch_s.at[i - 1], recv_sem=ch_r.at[i - 1],
            device_id=(dp, at_pair(to) * 4 + quad, p), device_id_type=MESH,
        )


    lower_tri = (iota((TOK, TOK), 0) < iota((TOK, TOK), 1)).astype(F32).astype(BF16)
    segment = iota((SEG, TOK), 0).astype(F32)
    row16 = iota((16, TOK), 0)
    names16 = (
        ((row16 >> 2) - (row16 & 1) + (pair + PAIRS - 1)) % PAIRS * 4 + (row16 & 3)
    ).astype(F32)
    shift = (0, 4, -4, 8)

    def fill(i, k, g):
        name = at_pair(lax.div(k, 4) - 1 - lax.rem(k, 2)) * 4 + lax.rem(k, 4)
        return name, pltpu.make_async_remote_copy(
            src_ref=sbuf.at[i, k], dst_ref=rbuf.at[g, quad], send_sem=f_s.at[i], recv_sem=f_r.at[g],
            device_id=(dp, name, p), device_id_type=MESH,
        )

    def select(i):
        g = at_pair(shift[i])
        x = jnp.concatenate([src[i, 0:TOK, :], src[i, TOK:2 * TOK, :]], axis=1)
        m16 = src[i, 2 * TOK:BLOCK, :].astype(F32)
        match = jnp.zeros((16, TOK), F32)
        gate = jnp.zeros((16, TOK), F32)
        for k in range(8):
            hit = m16[k:k + 1] == names16
            match = match + jnp.where(hit, 1.0, 0.0)
            gate = gate + jnp.where(hit, m16[8 + k:9 + k], 0.0)
        counts = jnp.dot(match.astype(BF16), lower_tri, preferred_element_type=F32)
        key = jnp.where(match > 0.5, counts, -1.0)
        pick = jnp.concatenate(
            [jnp.where(segment == key[k:k + 1], gate[k:k + 1], 0.0) for k in range(16)], axis=0
        ).astype(BF16)
        rows = jnp.dot(pick, x, preferred_element_type=F32)
        for k in range(16):
            r = rows[k * SEG:(k + 1) * SEG]
            sbuf[i, k] = jnp.concatenate([r[:, :half], r[:, half:]], axis=0).astype(BF16)

        def send(k, carry):
            name, copy = fill(i, k, g)

            @pl.when(name != e)
            def _():
                copy.start()
            return carry

        lax.fori_loop(0, 16, send, 0)
        pltpu.make_async_copy(sbuf.at[i, 4 * (1 + yh) + quad], rbuf.at[g, quad], f_r.at[g]).start()

    select(0)
    chain(1).start()
    chain(2).start()

    for copy in loads[3:]:
        copy.wait()

    def out_rows(i, carry):
        r = pl.multiple_of(i * 320, 320)
        prod = jnp.dot(st_v[pl.ds(r, 320), :], w_v[...], preferred_element_type=F32)
        eo[pl.ds(i * 4, 4)] = prod.reshape(4, ROWS, cols)
        return carry

    lax.fori_loop(0, 4, out_rows, 0)

    c_id, r_id = iota((2 * ROWS, 4 * PACK), 1), iota((2 * ROWS, 4 * PACK), 0)
    block = (
        (c_id >= PACK).astype(jnp.int32) + (c_id >= 2 * PACK).astype(jnp.int32)
        + (c_id >= 3 * PACK).astype(jnp.int32)
    )
    inside = c_id - block * PACK
    right = (inside >= SEG).astype(jnp.int32)
    slot_id = inside - right * SEG
    place = jnp.where(
        (slot_id < CAP) & (right * ROWS + block * CAP + slot_id == r_id), 1.0, 0.0
    ).astype(BF16)

    def group_of(j):
        i, r = lax.div(j, 4), lax.rem(j, 4)
        delta = jnp.where(r == 2, -1, jnp.where(r == 3, 2, r)) * (1 - 2 * yh)
        off = jnp.where(i == 1, 4, jnp.where(i == 2, -4, jnp.where(i == 3, 8, 0)))
        return lax.rem(pair - delta + off + 2 * PAIRS, PAIRS)

    wide = width // 2

    def core_copy(g, w):
        h, c = lax.div(g, 2), pl.ds(w * wide, wide)
        return pltpu.make_async_remote_copy(
            src_ref=pb.at[g, :, c], dst_ref=cr.at[h, :, c], send_sem=c_s.at[h, w], recv_sem=c_r.at[h, w],
            device_id=(dp, e, yl * 2 + (1 - core)), device_id_type=MESH,
        )

    def score_copy(g, b):
        return pltpu.make_async_remote_copy(
            src_ref=srow.at[g], dst_ref=rtab.at[e], send_sem=sc_s, recv_sem=sc_r,
            device_id=(dp, b, p), device_id_type=MESH,
        )

    diagonal = iota((ROWS, 128), 0) == iota((ROWS, 128), 1)

    def multiply(j):
        g = group_of(j)
        pltpu.make_async_copy(rbuf.at[g], rbuf.at[g], f_r.at[g]).wait()
        both = jnp.dot(place, rbuf[g].reshape(4 * PACK, half), preferred_element_type=F32)
        rr = jnp.concatenate([both[:ROWS], both[ROWS:]], axis=1).astype(BF16)
        rt[g] = rr
        for n in range(width // 256):
            part = lax.dot_general(
                rr, w_v[n * 256:(n + 1) * 256, :], (((1,), (1,)), ((), ())),
                preferred_element_type=F32,
            )
            pb[g, :, n * 256:(n + 1) * 256] = part.astype(BF16)
            if (n + 1) * 256 % wide == 0:
                @pl.when(lax.rem(g, 2) != core)
                def _():
                    core_copy(g, n * 256 // wide).start()

        total = jnp.sum(rr.astype(F32) * eo[g], axis=1, keepdims=True)
        srow[g] = jnp.sum(jnp.where(diagonal, total, 0.0), axis=0, keepdims=True)
        for q in range(4):
            b = 4 * g + q

            @pl.when(b != e)
            def _():
                score_copy(g, b).start()

            @pl.when(b == e)
            def _():
                rtab[e] = srow[g]

    def y_copy(h, w):
        c = pl.ds(w * wide, wide)
        return pltpu.make_async_remote_copy(
            src_ref=xs.at[h, :, c], dst_ref=yb.at[h, :, c], send_sem=y_s.at[h, w], recv_sem=y_r.at[h, w],
            device_id=(dp, e, (1 - yl) * 2 + core), device_id_type=MESH,
        )

    def x_copy(g, w):
        c = pl.ds(w * wide, wide)
        owner = lax.div(g, 4)
        place_x = jnp.maximum(lax.rem(dp - owner + 4, 4) - 1, 0)
        h = lax.div(g, 2)
        return pltpu.make_async_remote_copy(
            src_ref=xs.at[h, :, c], dst_ref=xr.at[place_x, :, c],
            send_sem=x_s.at[h, w], recv_sem=x_r.at[place_x, w],
            device_id=(owner, e, p), device_id_type=MESH,
        )

    def roles(g):
        mine = lax.rem(g, 2) == core
        row = lax.div(lax.rem(g, 4), 2) == yl
        return mine & jnp.logical_not(row), mine & row, mine & row & (lax.div(g, 4) != dp)

    step = width // 4

    def put_down(h, w, refs):
        for n in range(2 * w, 2 * w + 2):
            c = slice(n * step, (n + 1) * step)
            t = refs[0][:, c].astype(F32)
            for ref in refs[1:]:
                t = t + ref[:, c].astype(F32)
            xs[h, :, c] = t.astype(BF16)

    def along_y(j):
        g = group_of(j)
        h = lax.div(g, 2)
        gives, _, _ = roles(g)

        @pl.when(gives)
        def _():
            for w in range(2):
                core_copy(g, w).wait_recv()
                put_down(h, w, (pb.at[g], cr.at[h]))
                y_copy(h, w).start()

    def along_x(j):
        g = group_of(j)
        h = lax.div(g, 2)
        _, keeps, passes = roles(g)

        for w in range(2):
            @pl.when(keeps)
            def _():
                core_copy(g, w).wait_recv()
                y_copy(h, w).wait_recv()

            @pl.when(passes)
            def _():
                put_down(h, w, (pb.at[g], cr.at[h], yb.at[h]))
                x_copy(g, w).start()

    def down(i):
        gs = [group_of(4 * i + r) for r in range(4)]
        rows = jnp.concatenate([rt[g] for g in gs], axis=0)
        for n in range(width // 256):
            c = slice(n * 256, (n + 1) * 256)
            stash = jnp.concatenate(
                [st_v[pl.ds(pl.multiple_of(g * ROWS, 16), ROWS), c] for g in gs], axis=0
            )
            part = lax.dot_general(
                stash, rows, (((0,), (0,)), ((), ())), preferred_element_type=F32
            )
            if i > 0:
                part = part + acc[c, :]
            if i < 3:
                acc[c, :] = part
            else:
                dg_ref[0, c, :] = part.astype(BF16)

    def body(j, carry):
        @pl.when(j == 4)
        def _():
            along_y(j - 1)
            down(0)
            chain(1).wait_recv()
            chain(3).start()
            chain(2).wait_recv()
            chain(4).start()
            select(1)
            select(2)

        @pl.when(j == 8)
        def _():
            along_y(j - 1)
            down(1)
            chain(3).wait_recv()
            chain(4).wait_recv()
            select(3)

        @pl.when(j == 12)
        def _():
            along_y(j - 1)
            down(2)

        multiply(j)

        @pl.when((j != 0) & (j != 4) & (j != 8) & (j != 12))
        def _():
            along_y(j - 1)

        @pl.when(j >= 4)
        def _():
            along_x(j - 4)

        return carry

    lax.fori_loop(0, 16, body, 0)

    along_y(15)
    down(3)
    for j in range(12, 16):
        along_x(j)

    m16 = src[0, 2 * TOK:BLOCK, :].astype(F32)
    names = iota((NAMES, TOK), 0).astype(F32)
    hits = [jnp.where(names == m16[k:k + 1, :], 1.0, 0.0) for k in range(8)]
    named = functools.reduce(lambda a, b: a + b, hits)
    counts = jnp.dot(named.astype(BF16), lower_tri, preferred_element_type=F32)
    lanes = iota((128, TOK), 0).astype(F32)
    first = (quad * CAP).astype(F32)
    pltpu.make_async_copy(
        rtab.at[pl.ds(0, NAMES - 1)], rtab.at[pl.ds(0, NAMES - 1)], sc_r
    ).wait()
    table = rtab[...].reshape(NAMES, 128)
    high = table.astype(BF16)
    low = (table - high.astype(F32)).astype(BF16)
    out = []
    for k in range(8):
        slot = jnp.sum(hits[k] * counts, axis=0, keepdims=True) + first
        one = hits[k].astype(BF16)
        values = lax.dot_general(
            high, one, (((0,), (0,)), ((), ())), preferred_element_type=F32
        ) + lax.dot_general(low, one, (((0,), (0,)), ((), ())), preferred_element_type=F32)
        out.append(jnp.sum(jnp.where(lanes == slot, values, 0.0), axis=0, keepdims=True))
    ar[me] = jnp.concatenate(out, axis=0)

    def spread_one(i, carry):
        @pl.when(i != me)
        def _():
            pltpu.make_async_remote_copy(
                src_ref=ar.at[me], dst_ref=ar.at[me], send_sem=ar_s, recv_sem=ar_r,
                device_id=(lax.div(i, 4), e, lax.rem(i, 4)), device_id_type=MESH,
            ).start()
        return carry

    lax.fori_loop(0, 16, spread_one, 0)

    h = lax.div(me, 2)
    for n in range(4):
        if n % 2 == 0:
            for i in range(3):
                ref = xr.at[i, :, pl.ds(n // 2 * wide, wide)]
                pltpu.make_async_copy(ref, ref, x_r.at[i, n // 2]).wait()
        c = slice(n * step, (n + 1) * step)
        t = pb[me, :, c].astype(F32)
        for ref in (cr.at[h], yb.at[h], xr.at[0], xr.at[1], xr.at[2]):
            t = t + ref[:, c].astype(F32)
        hg_ref[0, :, c] = t.astype(BF16)

    pltpu.make_async_copy(ar.at[pl.ds(0, 15)], ar.at[pl.ds(0, 15)], ar_r).wait()
    gg_ref[...] = jnp.sum(ar[...], axis=0) / m16[8:16]

    for i in range(1, 5):
        chain(i).wait_send()
    for i in range(4):
        pltpu.make_async_copy(sbuf.at[i, pl.ds(0, 15)], sbuf.at[i, pl.ds(0, 15)], f_s.at[i]).wait()

    def sent(g, carry):
        gives, _, passes = roles(g)

        for w in range(2):
            @pl.when(lax.rem(g, 2) != core)
            def _():
                core_copy(g, w).wait_send()

            @pl.when(gives)
            def _():
                y_copy(lax.div(g, 2), w).wait_send()

            @pl.when(passes)
            def _():
                x_copy(g, w).wait_send()

        return carry

    lax.fori_loop(0, 16, sent, 0)
    pltpu.make_async_copy(
        rtab.at[pl.ds(0, NAMES - 1)], rtab.at[pl.ds(0, NAMES - 1)], sc_s
    ).wait()
    pltpu.make_async_copy(ar.at[pl.ds(0, 15)], ar.at[pl.ds(0, 15)], ar_s).wait()


def local(dout, expert_ids, gates, down_weight, hidden_stash):
    _, width, cols = down_weight.shape
    slots = hidden_stash.shape[1]
    vmem = pl.BlockSpec(memory_space=pltpu.VMEM)
    hbm = pl.BlockSpec(memory_space=pl.ANY)
    dma = pltpu.SemaphoreType.DMA
    meta = jnp.concatenate([expert_ids.T.astype(BF16), gates.T], axis=0)
    hg, dg, gg = pl.pallas_call(
        kernel,
        out_shape=(
            jax.ShapeDtypeStruct((1, ROWS, width), BF16),
            jax.ShapeDtypeStruct((1, width, cols), BF16),
            jax.ShapeDtypeStruct((8, TOK), F32),
        ),
        in_specs=[hbm, hbm, hbm, hbm],
        out_specs=(vmem, vmem, vmem),
        scratch_shapes=[
            pltpu.VMEM((4, BLOCK, cols // 2), BF16),
            pltpu.VMEM((width, cols), BF16),
            pltpu.VMEM((slots, width), BF16),
            pltpu.VMEM((4, 16, PACK, cols // 2), BF16),
            pltpu.VMEM((PAIRS, 4, PACK, cols // 2), BF16),
            pltpu.VMEM((16, ROWS, cols), BF16),
            pltpu.VMEM((16, ROWS, cols), F32),
            pltpu.VMEM((16, ROWS, width), BF16),
            pltpu.VMEM((8, ROWS, width), BF16),
            pltpu.VMEM((8, ROWS, width), BF16),
            pltpu.VMEM((8, ROWS, width), BF16),
            pltpu.VMEM((3, ROWS, width), BF16),
            pltpu.VMEM((width, cols), F32),
            pltpu.VMEM((16, 1, 128), F32),
            pltpu.VMEM((NAMES, 1, 128), F32),
            pltpu.VMEM((16, 8, TOK), F32),
            dma((5,)),
            dma((4,)),
            dma((4,)),
            dma((4,)),
            dma((16,)),
            dma((8, 2)),
            dma((8, 2)),
            dma((8, 2)),
            dma((8, 2)),
            dma((8, 2)),
            dma((3, 2)),
            dma(()),
            dma(()),
            dma(()),
            dma(()),
        ],
        compiler_params=pltpu.CompilerParams(
            collective_id=0, has_side_effects=True, vmem_limit_bytes=60 * 2**20
        ),
        cost_estimate=pl.CostEstimate(
            flops=6 * slots * width * cols, bytes_accessed=6 * 2**20, transcendentals=0
        ),
    )(dout, meta, down_weight[0], hidden_stash[0])
    return hg, dg, gg.T


def solution(mesh):
    in_specs = (
        P("expert", ("dp", "pipe")),
        P("expert", None),
        P("expert", None),
        P("expert", None, ("dp", "pipe")),
        P("expert", None, None),
    )
    out_specs = (
        P("expert", ("dp", "pipe"), None),
        P("expert", None, ("dp", "pipe")),
        P("expert", None),
    )
    return jax.shard_map(local, mesh=mesh, in_specs=in_specs, out_specs=out_specs, check_vma=False)
```

```python
import functools

import jax
import jax.numpy as jnp
from jax import lax
from jax.experimental import pallas as pl
from jax.experimental.pallas import tpu as pltpu
from jax.sharding import PartitionSpec as P

MESH = pl.DeviceIdType.MESH
F32 = jnp.float32
BF16 = jnp.bfloat16
PAIRS = 16
NAMES = 4 * PAIRS
TOK = 128
CAP = 20
ROWS = 4 * CAP
SEG = 24
PACK = 2 * SEG
META = 16
BLOCK = 2 * TOK + META


def iota(shape, dim):
    return lax.broadcasted_iota(jnp.int32, shape, dim)


def kernel(
    dout_hbm, ids_hbm, gates_hbm, w_hbm, st_hbm, hg_ref, dg_ref, gg_ref,
    ids_v, gates_v, src, w_v, st_v, sbuf, rbuf, rt, eo, pb, cr, xs, yb, xr, acc, srow, rtab, ar,
    load_sem, ch_s, ch_r, f_s, f_r, c_s, c_r, y_s, y_r, x_s, x_r, sc_s, sc_r, ar_s, ar_r,
):
    dp, e, p = lax.axis_index("dp"), lax.axis_index("expert"), lax.axis_index("pipe")
    pair, quad = lax.div(e, 4), lax.rem(e, 4)
    yh, yl, core = lax.rem(e, 2), lax.div(p, 2), lax.rem(p, 2)
    me = dp * 4 + p
    width, cols = w_v.shape
    half = cols // 2

    def at_pair(d):
        return lax.rem(pair + d + PAIRS, PAIRS)

    loads = [
        pltpu.make_async_copy(dout_hbm.at[:, pl.ds(0, half)], src.at[0, pl.ds(0, TOK)], load_sem.at[0]),
        pltpu.make_async_copy(dout_hbm.at[:, pl.ds(half, half)], src.at[0, pl.ds(TOK, TOK)], load_sem.at[1]),
        pltpu.make_async_copy(ids_hbm, ids_v, load_sem.at[2]),
        pltpu.make_async_copy(gates_hbm, gates_v, load_sem.at[5]),
        pltpu.make_async_copy(w_hbm, w_v, load_sem.at[3]),
        pltpu.make_async_copy(st_hbm, st_v, load_sem.at[4]),
    ]
    for copy in loads:
        copy.start()

    barrier = pltpu.get_barrier_semaphore()

    def greet(name):
        pl.semaphore_signal(barrier, inc=1, device_id=(dp, name, p), device_id_type=MESH)

    greet(at_pair(4) * 4 + quad)
    greet(at_pair(-4) * 4 + quad)

    def greet_near(k, carry):
        name = at_pair(lax.div(k, 4) - 2 + yh) * 4 + lax.rem(k, 4)

        @pl.when(name != e)
        def _():
            greet(name)
        return carry

    def greet_group(i, carry):
        @pl.when(i != me)
        def _():
            pl.semaphore_signal(
                barrier, inc=1, device_id=(lax.div(i, 4), e, lax.rem(i, 4)), device_id_type=MESH
            )
        return carry

    lax.fori_loop(0, 16, greet_near, 0)
    lax.fori_loop(0, 16, greet_group, 0)
    for copy in loads[:4]:
        copy.wait()
    src[0, 2 * TOK:BLOCK, :] = jnp.concatenate(
        [ids_v[...].astype(F32), gates_v[...].astype(F32)], axis=0
    ).astype(BF16)
    pl.semaphore_wait(barrier, 2 + 15 + 15)

    def chain(i):
        frm, to, dst, lo, size = (
            (0, -4, 1, 0, BLOCK), (0, 4, 2, 0, BLOCK),
            (1, -4, 3, TOK, BLOCK - TOK), (2, 4, 3, 0, TOK),
        )[i - 1]
        return pltpu.make_async_remote_copy(
            src_ref=src.at[frm, pl.ds(lo, size)], dst_ref=src.at[dst, pl.ds(lo, size)],
            send_sem=ch_s.at[i - 1], recv_sem=ch_r.at[i - 1],
            device_id=(dp, at_pair(to) * 4 + quad, p), device_id_type=MESH,
        )


    lower_tri = (iota((TOK, TOK), 0) < iota((TOK, TOK), 1)).astype(F32).astype(BF16)
    segment = iota((SEG, TOK), 0).astype(F32)
    row16 = iota((16, TOK), 0)
    names16 = (
        ((row16 >> 2) - (row16 & 1) + (pair + PAIRS - 1)) % PAIRS * 4 + (row16 & 3)
    ).astype(F32)
    shift = (0, 4, -4, 8)

    def fill(i, k, g):
        name = at_pair(lax.div(k, 4) - 1 - lax.rem(k, 2)) * 4 + lax.rem(k, 4)
        return name, pltpu.make_async_remote_copy(
            src_ref=sbuf.at[i, k], dst_ref=rbuf.at[g, quad], send_sem=f_s.at[i], recv_sem=f_r.at[g],
            device_id=(dp, name, p), device_id_type=MESH,
        )

    def select(i):
        g = at_pair(shift[i])
        x = jnp.concatenate([src[i, 0:TOK, :], src[i, TOK:2 * TOK, :]], axis=1)
        m16 = src[i, 2 * TOK:BLOCK, :].astype(F32)
        match = jnp.zeros((16, TOK), F32)
        gate = jnp.zeros((16, TOK), F32)
        for k in range(8):
            hit = m16[k:k + 1] == names16
            match = match + jnp.where(hit, 1.0, 0.0)
            gate = gate + jnp.where(hit, m16[8 + k:9 + k], 0.0)
        counts = jnp.dot(match.astype(BF16), lower_tri, preferred_element_type=F32)
        key = jnp.where(match > 0.5, counts, -1.0)
        pick = jnp.concatenate(
            [jnp.where(segment == key[k:k + 1], gate[k:k + 1], 0.0) for k in range(16)], axis=0
        ).astype(BF16)
        rows = jnp.dot(pick, x, preferred_element_type=F32)
        for k in range(16):
            r = rows[k * SEG:(k + 1) * SEG]
            sbuf[i, k] = jnp.concatenate([r[:, :half], r[:, half:]], axis=0).astype(BF16)

        def send(k, carry):
            name, copy = fill(i, k, g)

            @pl.when(name != e)
            def _():
                copy.start()
            return carry

        lax.fori_loop(0, 16, send, 0)
        pltpu.make_async_copy(sbuf.at[i, 4 * (1 + yh) + quad], rbuf.at[g, quad], f_r.at[g]).start()

    select(0)
    chain(1).start()
    chain(2).start()

    for copy in loads[4:]:
        copy.wait()

    def out_rows(i, carry):
        r = pl.multiple_of(i * 320, 320)
        prod = jnp.dot(st_v[pl.ds(r, 320), :], w_v[...], preferred_element_type=F32)
        eo[pl.ds(i * 4, 4)] = prod.reshape(4, ROWS, cols)
        return carry

    lax.fori_loop(0, 4, out_rows, 0)

    c_id, r_id = iota((2 * ROWS, 4 * PACK), 1), iota((2 * ROWS, 4 * PACK), 0)
    block = (
        (c_id >= PACK).astype(jnp.int32) + (c_id >= 2 * PACK).astype(jnp.int32)
        + (c_id >= 3 * PACK).astype(jnp.int32)
    )
    inside = c_id - block * PACK
    right = (inside >= SEG).astype(jnp.int32)
    slot_id = inside - right * SEG
    place = jnp.where(
        (slot_id < CAP) & (right * ROWS + block * CAP + slot_id == r_id), 1.0, 0.0
    ).astype(BF16)

    def group_of(j):
        i, r = lax.div(j, 4), lax.rem(j, 4)
        delta = jnp.where(r == 2, -1, jnp.where(r == 3, 2, r)) * (1 - 2 * yh)
        off = jnp.where(i == 1, 4, jnp.where(i == 2, -4, jnp.where(i == 3, 8, 0)))
        return lax.rem(pair - delta + off + 2 * PAIRS, PAIRS)

    wide = width // 2

    def core_copy(g, w):
        h, c = lax.div(g, 2), pl.ds(w * wide, wide)
        return pltpu.make_async_remote_copy(
            src_ref=pb.at[g, :, c], dst_ref=cr.at[h, :, c], send_sem=c_s.at[h, w], recv_sem=c_r.at[h, w],
            device_id=(dp, e, yl * 2 + (1 - core)), device_id_type=MESH,
        )

    def score_copy(g, b):
        return pltpu.make_async_remote_copy(
            src_ref=srow.at[g], dst_ref=rtab.at[e], send_sem=sc_s, recv_sem=sc_r,
            device_id=(dp, b, p), device_id_type=MESH,
        )

    diagonal = iota((ROWS, 128), 0) == iota((ROWS, 128), 1)

    def multiply(j):
        g = group_of(j)
        pltpu.make_async_copy(rbuf.at[g], rbuf.at[g], f_r.at[g]).wait()
        both = jnp.dot(place, rbuf[g].reshape(4 * PACK, half), preferred_element_type=F32)
        rr = jnp.concatenate([both[:ROWS], both[ROWS:]], axis=1).astype(BF16)
        rt[g] = rr
        for n in range(width // 256):
            part = lax.dot_general(
                rr, w_v[n * 256:(n + 1) * 256, :], (((1,), (1,)), ((), ())),
                preferred_element_type=F32,
            )
            pb[g, :, n * 256:(n + 1) * 256] = part.astype(BF16)
            if (n + 1) * 256 % wide == 0:
                @pl.when(lax.rem(g, 2) != core)
                def _():
                    core_copy(g, n * 256 // wide).start()

        total = jnp.sum(rr.astype(F32) * eo[g], axis=1, keepdims=True)
        srow[g] = jnp.sum(jnp.where(diagonal, total, 0.0), axis=0, keepdims=True)
        for q in range(4):
            b = 4 * g + q

            @pl.when(b != e)
            def _():
                score_copy(g, b).start()

            @pl.when(b == e)
            def _():
                rtab[e] = srow[g]

    def y_copy(h, w):
        c = pl.ds(w * wide, wide)
        return pltpu.make_async_remote_copy(
            src_ref=xs.at[h, :, c], dst_ref=yb.at[h, :, c], send_sem=y_s.at[h, w], recv_sem=y_r.at[h, w],
            device_id=(dp, e, (1 - yl) * 2 + core), device_id_type=MESH,
        )

    def x_copy(g, w):
        c = pl.ds(w * wide, wide)
        owner = lax.div(g, 4)
        place_x = jnp.maximum(lax.rem(dp - owner + 4, 4) - 1, 0)
        h = lax.div(g, 2)
        return pltpu.make_async_remote_copy(
            src_ref=xs.at[h, :, c], dst_ref=xr.at[place_x, :, c],
            send_sem=x_s.at[h, w], recv_sem=x_r.at[place_x, w],
            device_id=(owner, e, p), device_id_type=MESH,
        )

    def roles(g):
        mine = lax.rem(g, 2) == core
        row = lax.div(lax.rem(g, 4), 2) == yl
        return mine & jnp.logical_not(row), mine & row, mine & row & (lax.div(g, 4) != dp)

    step = width // 4

    def put_down(h, w, refs):
        for n in range(2 * w, 2 * w + 2):
            c = slice(n * step, (n + 1) * step)
            t = refs[0][:, c].astype(F32)
            for ref in refs[1:]:
                t = t + ref[:, c].astype(F32)
            xs[h, :, c] = t.astype(BF16)

    def along_y(j):
        g = group_of(j)
        h = lax.div(g, 2)
        gives, _, _ = roles(g)

        @pl.when(gives)
        def _():
            for w in range(2):
                core_copy(g, w).wait_recv()
                put_down(h, w, (pb.at[g], cr.at[h]))
                y_copy(h, w).start()

    def along_x(j):
        g = group_of(j)
        h = lax.div(g, 2)
        _, keeps, passes = roles(g)

        for w in range(2):
            @pl.when(keeps)
            def _():
                core_copy(g, w).wait_recv()
                y_copy(h, w).wait_recv()

            @pl.when(passes)
            def _():
                put_down(h, w, (pb.at[g], cr.at[h], yb.at[h]))
                x_copy(g, w).start()

    def down(i):
        gs = [group_of(4 * i + r) for r in range(4)]
        rows = jnp.concatenate([rt[g] for g in gs], axis=0)
        for n in range(width // 256):
            c = slice(n * 256, (n + 1) * 256)
            stash = jnp.concatenate(
                [st_v[pl.ds(pl.multiple_of(g * ROWS, 16), ROWS), c] for g in gs], axis=0
            )
            part = lax.dot_general(
                stash, rows, (((0,), (0,)), ((), ())), preferred_element_type=F32
            )
            if i > 0:
                part = part + acc[c, :]
            if i < 3:
                acc[c, :] = part
            else:
                dg_ref[0, c, :] = part.astype(BF16)

    def body(j, carry):
        @pl.when(j == 4)
        def _():
            along_y(j - 1)
            down(0)
            chain(1).wait_recv()
            chain(3).start()
            chain(2).wait_recv()
            chain(4).start()
            select(1)
            select(2)
            for k in range(4):
                along_x(k)

        @pl.when(j == 8)
        def _():
            along_y(j - 1)
            down(1)
            chain(3).wait_recv()
            chain(4).wait_recv()
            select(3)

        @pl.when(j == 12)
        def _():
            along_y(j - 1)
            down(2)

        multiply(j)

        @pl.when((j != 0) & (j != 4) & (j != 8) & (j != 12))
        def _():
            along_y(j - 1)

        @pl.when(j >= 8)
        def _():
            along_x(j - 4)

        return carry

    lax.fori_loop(0, 16, body, 0)

    along_y(15)
    down(3)
    for j in range(12, 16):
        along_x(j)

    m16 = src[0, 2 * TOK:BLOCK, :].astype(F32)
    names = iota((NAMES, TOK), 0).astype(F32)
    hits = [jnp.where(names == m16[k:k + 1, :], 1.0, 0.0) for k in range(8)]
    named = functools.reduce(lambda a, b: a + b, hits)
    counts = jnp.dot(named.astype(BF16), lower_tri, preferred_element_type=F32)
    lanes = iota((128, TOK), 0).astype(F32)
    first = (quad * CAP).astype(F32)
    pltpu.make_async_copy(
        rtab.at[pl.ds(0, NAMES - 1)], rtab.at[pl.ds(0, NAMES - 1)], sc_r
    ).wait()
    table = rtab[...].reshape(NAMES, 128)
    high = table.astype(BF16)
    low = (table - high.astype(F32)).astype(BF16)
    out = []
    for k in range(8):
        slot = jnp.sum(hits[k] * counts, axis=0, keepdims=True) + first
        one = hits[k].astype(BF16)
        values = lax.dot_general(
            high, one, (((0,), (0,)), ((), ())), preferred_element_type=F32
        ) + lax.dot_general(low, one, (((0,), (0,)), ((), ())), preferred_element_type=F32)
        out.append(jnp.sum(jnp.where(lanes == slot, values, 0.0), axis=0, keepdims=True))
    ar[me] = jnp.concatenate(out, axis=0)

    def spread_one(i, carry):
        @pl.when(i != me)
        def _():
            pltpu.make_async_remote_copy(
                src_ref=ar.at[me], dst_ref=ar.at[me], send_sem=ar_s, recv_sem=ar_r,
                device_id=(lax.div(i, 4), e, lax.rem(i, 4)), device_id_type=MESH,
            ).start()
        return carry

    lax.fori_loop(0, 16, spread_one, 0)

    h = lax.div(me, 2)
    for n in range(4):
        if n % 2 == 0:
            for i in range(3):
                ref = xr.at[i, :, pl.ds(n // 2 * wide, wide)]
                pltpu.make_async_copy(ref, ref, x_r.at[i, n // 2]).wait()
        c = slice(n * step, (n + 1) * step)
        t = pb[me, :, c].astype(F32)
        for ref in (cr.at[h], yb.at[h], xr.at[0], xr.at[1], xr.at[2]):
            t = t + ref[:, c].astype(F32)
        hg_ref[0, :, c] = t.astype(BF16)

    pltpu.make_async_copy(ar.at[pl.ds(0, 15)], ar.at[pl.ds(0, 15)], ar_r).wait()
    gg_ref[...] = jnp.sum(ar[...], axis=0) / m16[8:16]

    for i in range(1, 5):
        chain(i).wait_send()
    for i in range(4):
        pltpu.make_async_copy(sbuf.at[i, pl.ds(0, 15)], sbuf.at[i, pl.ds(0, 15)], f_s.at[i]).wait()

    def sent(g, carry):
        gives, _, passes = roles(g)

        for w in range(2):
            @pl.when(lax.rem(g, 2) != core)
            def _():
                core_copy(g, w).wait_send()

            @pl.when(gives)
            def _():
                y_copy(lax.div(g, 2), w).wait_send()

            @pl.when(passes)
            def _():
                x_copy(g, w).wait_send()

        return carry

    lax.fori_loop(0, 16, sent, 0)
    pltpu.make_async_copy(
        rtab.at[pl.ds(0, NAMES - 1)], rtab.at[pl.ds(0, NAMES - 1)], sc_s
    ).wait()
    pltpu.make_async_copy(ar.at[pl.ds(0, 15)], ar.at[pl.ds(0, 15)], ar_s).wait()


def local(dout, expert_ids, gates, down_weight, hidden_stash):
    _, width, cols = down_weight.shape
    slots = hidden_stash.shape[1]
    vmem = pl.BlockSpec(memory_space=pltpu.VMEM)
    hbm = pl.BlockSpec(memory_space=pl.ANY)
    dma = pltpu.SemaphoreType.DMA
    hg, dg, gg = pl.pallas_call(
        kernel,
        out_shape=(
            jax.ShapeDtypeStruct((1, ROWS, width), BF16),
            jax.ShapeDtypeStruct((1, width, cols), BF16),
            jax.ShapeDtypeStruct((8, TOK), F32),
        ),
        in_specs=[hbm, hbm, hbm, hbm, hbm],
        out_specs=(vmem, vmem, vmem),
        scratch_shapes=[
            pltpu.VMEM((8, TOK), jnp.int32),
            pltpu.VMEM((8, TOK), BF16),
            pltpu.VMEM((4, BLOCK, cols // 2), BF16),
            pltpu.VMEM((width, cols), BF16),
            pltpu.VMEM((slots, width), BF16),
            pltpu.VMEM((4, 16, PACK, cols // 2), BF16),
            pltpu.VMEM((PAIRS, 4, PACK, cols // 2), BF16),
            pltpu.VMEM((16, ROWS, cols), BF16),
            pltpu.VMEM((16, ROWS, cols), F32),
            pltpu.VMEM((16, ROWS, width), BF16),
            pltpu.VMEM((8, ROWS, width), BF16),
            pltpu.VMEM((8, ROWS, width), BF16),
            pltpu.VMEM((8, ROWS, width), BF16),
            pltpu.VMEM((3, ROWS, width), BF16),
            pltpu.VMEM((width, cols), F32),
            pltpu.VMEM((16, 1, 128), F32),
            pltpu.VMEM((NAMES, 1, 128), F32),
            pltpu.VMEM((16, 8, TOK), F32),
            dma((6,)),
            dma((4,)),
            dma((4,)),
            dma((4,)),
            dma((16,)),
            dma((8, 2)),
            dma((8, 2)),
            dma((8, 2)),
            dma((8, 2)),
            dma((8, 2)),
            dma((3, 2)),
            dma(()),
            dma(()),
            dma(()),
            dma(()),
        ],
        compiler_params=pltpu.CompilerParams(
            collective_id=0, has_side_effects=True, vmem_limit_bytes=50 * 2**20
        ),
        cost_estimate=pl.CostEstimate(
            flops=6 * slots * width * cols, bytes_accessed=6 * 2**20, transcendentals=0
        ),
    )(dout, expert_ids.T, gates.T, down_weight[0], hidden_stash[0])
    return hg, dg, gg.T


def solution(mesh):
    in_specs = (
        P("expert", ("dp", "pipe")),
        P("expert", None),
        P("expert", None),
        P("expert", None, ("dp", "pipe")),
        P("expert", None, None),
    )
    out_specs = (
        P("expert", ("dp", "pipe"), None),
        P("expert", None, ("dp", "pipe")),
        P("expert", None),
    )
    return jax.shard_map(local, mesh=mesh, in_specs=in_specs, out_specs=out_specs, check_vma=False)
```
